32 devices in a mesh: inst: 2 (over x), period: 2 (over core), row: 8 (over z, y).
Axes of the slice: x: 2, y: 2, z: 4, core: 2. Of those that a mesh axis runs over, the one named last changes fastest.
Arguments:
- linking: bfloat16 [24576, 4096], P(('inst', 'period', 'row')), parts along dimension 0, may hold values from -0.28867513 to 0.28867513
- tile_mask: int32 [192, 32], P(('inst', 'period', 'row')), parts along dimension 0, may hold values 0 or 1
- scaling: float32 [24576], P(('inst', 'period', 'row')), parts along dimension 0, may hold values from 0.1 to 10
- link_diag: float32 [2048], P(('inst', 'row')), parts along dimension 0, may hold values from 0.5 to 2
Outputs:
- diag_factor: float32 [2048, 1024], P(('inst', 'row')), parts along dimension 0
- below_factor: float32 [6144, 1024], P(('inst', 'row')), parts along dimension 0
The draws below stay inside these ranges and needn't reach their ends.
There are 2 independent parts, one for each index of `inst`. The reference program is written for one: setup_inputs(seed, part) draws one part's arguments, and reference() takes and returns one part's arrays. A program takes and returns all parts, laid end to end along the dimension named above; each array names one. Nothing has to cross between parts.
All inputs are finite; a program needn't handle non-finite values. No bound on the sum of `tile_mask` on one device may be relied on, other than what follows from the above.
Results may differ from the reference program's by a relative error of at most 0.0038.
Values sent between devices are 32-bit elements; how exact they have to be, the bound alone decides.
No kernel may reach another device: no remote copies, remote signals or barrier semaphores. Data moves between devices by JAX's collectives and lax.ppermute only.
A program may use at most 128 MiB of HBM per device.

```python
import math
import jax
import jax.numpy as jnp
from jax import lax

LINK = 4096
PANEL = 1024
TILE = 128
ROW_DEV = 768
ROWS_ALL = 12288


def draw_linking(key, part):
    key_base = jax.random.fold_in(key, 11)
    key_share = jax.random.fold_in(key, 23)
    key_pair = jax.random.fold_in(key, 37)
    sigma = ROWS_ALL ** (-0.5)
    base = jnp.clip(jax.random.normal(key_base, (ROWS_ALL, LINK), jnp.float32), -6.0, 6.0)
    shared = jnp.clip(jax.random.normal(key_share, (ROWS_ALL,), jnp.float32), -4.0, 4.0)
    mixing = 0.7
    blocks = ROWS_ALL // ROW_DEV
    pairing = jax.random.permutation(key_pair, blocks)
    row_block = jnp.arange(ROWS_ALL, dtype=jnp.int32) // ROW_DEV
    col_block = jnp.arange(LINK, dtype=jnp.int32) // (LINK // blocks)
    spike = jnp.where(pairing[row_block][:, None] == col_block[None, :], 4.0, 1.0).astype(jnp.float32)
    in_panel = (jnp.arange(LINK, dtype=jnp.int32) < PANEL).astype(jnp.float32)
    values = (base * spike + mixing * shared[:, None] * in_panel[None, :]) * sigma
    values = jnp.clip(values, -32.0 * sigma, 32.0 * sigma)
    return values.astype(jnp.bfloat16)


def set_ends(array, key, low, high):
    extent = array.shape
    place = [jax.random.randint(jax.random.fold_in(key, axis), (), 0, extent[axis]) for axis in range(len(extent))]
    array = array.at[tuple(place)].set(low)
    longest = extent.index(max(extent))
    place[longest] = (place[longest] + 1) % extent[longest]
    return array.at[tuple(place)].set(high)


def levels(rng, dims, pieces, smallest, top_value):
    def one(axis_at, shards_of):
        steps = jax.random.uniform(jax.random.fold_in(jax.random.fold_in(rng, 6), axis_at), (shards_of,), jnp.float32, smallest / len(pieces), top_value / len(pieces))
        return jnp.repeat(jnp.exp(steps), dims[axis_at] // shards_of).reshape((-1,) + (1,) * (len(dims) - axis_at - 1))

    level = one(*pieces[0])
    for cut in pieces[1:]:
        level = level * one(*cut)
    return level


def setup_inputs(seed: int = 0, part: int = 0) -> dict:
    key_list = jax.random.split(jax.random.key(seed), 5)
    part_splits = jax.random.split(jax.random.fold_in(key_list[4], part), 5)
    return {
        "linking": draw_linking(jax.random.fold_in(jax.random.fold_in(key_list[4], part), 71), part),
        "tile_mask": set_ends((jax.random.randint(part_splits[1], (ROWS_ALL // TILE, LINK // TILE), 0, 2) < 1).astype(jnp.int32), jax.random.fold_in(part_splits[1], 1), 0, 1),
        "scaling": jnp.clip(jnp.exp(math.log(10.0) - 4.6051702 * jax.random.uniform(part_splits[2], (ROWS_ALL,), jnp.float32) ** levels(part_splits[2], (ROWS_ALL,), ((0, 16),), -0.2, 0.2)), 0.1, 10.0),
        "link_diag": jnp.clip(jnp.exp(math.log(2.0) - 1.3862944 * jax.random.uniform(part_splits[3], (PANEL,), jnp.float32) ** levels(part_splits[3], (PANEL,), ((0, 8),), -0.2, 0.2)), 0.5, 2.0),
    }


def expand_mask(lin_rows, mask_rows):
    row_count = lin_rows.shape[0]
    width_all = lin_rows.shape[1]
    spread = lin_rows.reshape(row_count // TILE, TILE, width_all // TILE, TILE) * mask_rows.astype(jnp.bfloat16)[:, None, :, None]
    return spread.reshape(row_count, width_all)

def reference(linking, tile_mask, scaling, link_diag):
    block_count = linking.shape[0] // ROW_DEV

    def add_block(totals, blk_index):
        row_start = blk_index * ROW_DEV
        lin_rows = lax.dynamic_slice_in_dim(linking, row_start, ROW_DEV, 0)
        mask_rows = lax.dynamic_slice_in_dim(tile_mask, blk_index * (ROW_DEV // TILE), ROW_DEV // TILE, 0)
        scale_rows = lax.dynamic_slice_in_dim(scaling, row_start, ROW_DEV, 0)
        masked = expand_mask(lin_rows, mask_rows)
        scaled = (scale_rows[:, None] * masked[:, :PANEL].astype(jnp.float32)).astype(jnp.bfloat16)
        return (totals + jnp.dot(masked.T.astype(jnp.float32), scaled.astype(jnp.float32), preferred_element_type=jnp.float32), None)
    panel, unused = lax.scan(add_block, jnp.zeros((LINK, PANEL), jnp.float32), jnp.arange(block_count, dtype=jnp.int32))
    upper = panel[:PANEL] + jnp.diag(link_diag)
    factor = jnp.linalg.cholesky(upper)
    below = lax.linalg.triangular_solve(factor, panel[PANEL:], left_side=False, lower=True, transpose_a=True)
    return (factor, below)
```

```python
import functools

import jax
import jax.numpy as jnp
from jax import lax
from jax.experimental import pallas as pl
from jax.experimental.pallas import tpu as pltpu
from jax.sharding import PartitionSpec as P

TILE = 128
SUB = 8
HIGH = lax.Precision.HIGHEST
VMEM = pl.BlockSpec(memory_space=pltpu.VMEM)
SMEM = pl.BlockSpec(memory_space=pltpu.SMEM)
ANY = pl.BlockSpec(memory_space=pl.ANY)
PARAMS = pltpu.CompilerParams(vmem_limit_bytes=48 << 20)


def dot(a, b, contract_a, contract_b):
    return lax.dot_general(
        a, b, (((contract_a,), (contract_b,)), ((), ())), precision=HIGH, preferred_element_type=jnp.float32
    )


def dot_rows(a, b):
    return lax.dot_general(a, b, (((0,), (0,)), ((), ())), preferred_element_type=jnp.float32)


def diag_kernel(core_ref, mask_ref, scale_ref, ridge_ref, lin_ref, send_ref, keep_ref, scaled_ref, masked, buf):
    rows, width = lin_ref.shape
    blocks = width // TILE
    half = TILE // 2
    for t in range(rows // TILE):
        lanes = slice(t * TILE, (t + 1) * TILE)
        factor = jnp.transpose(jnp.broadcast_to(scale_ref[t : t + 1, :], (TILE, TILE)))
        for i in range(blocks):
            cols = slice(i * TILE, (i + 1) * TILE)
            tile = lin_ref[lanes, cols].astype(jnp.float32) * mask_ref[t, i].astype(jnp.float32)
            masked[lanes, cols] = tile.astype(jnp.bfloat16)
            scaled_ref[lanes, cols] = (factor * tile).astype(jnp.bfloat16)
    eye = lax.broadcasted_iota(jnp.int32, (TILE, TILE), 0) == lax.broadcasted_iota(jnp.int32, (TILE, TILE), 1)
    start = 0
    for j in range(blocks):
        first = slice(j * TILE, (j + 1) * TILE)
        span = (blocks - j) * TILE
        buf[:, start : start + span] = 0.5 * (
            dot_rows(scaled_ref[:, first], masked[:, j * TILE :]) + dot_rows(masked[:, first], scaled_ref[:, j * TILE :])
        )
        buf[:, start : start + TILE] += jnp.where(eye, ridge_ref[j : j + 1, :], 0.0)
        start += span
    core = core_ref[0]
    keep_ref[...] = buf[pl.ds(pl.multiple_of(core * half, half), half), :]
    send_ref[...] = buf[pl.ds(pl.multiple_of((1 - core) * half, half), half), :]


def diag_products(core, tile_mask, scaling, ridge, linking, width):
    rows = linking.shape[0]
    blocks = width // TILE
    packed = blocks * (blocks + 1) // 2 * TILE
    half = jax.ShapeDtypeStruct((TILE // 2, packed), jnp.float32)
    return pl.pallas_call(
        diag_kernel,
        grid=(1,),
        out_shape=(half, half, jax.ShapeDtypeStruct((rows, width), jnp.bfloat16)),
        in_specs=[SMEM, SMEM, VMEM, VMEM, pl.BlockSpec((rows, width), lambda g: (0, 0))],
        out_specs=(VMEM, VMEM, VMEM),
        scratch_shapes=[pltpu.VMEM((rows, width), jnp.bfloat16), pltpu.VMEM((TILE, packed), jnp.float32)],
        compiler_params=PARAMS,
        name="diag_products",
    )(core, tile_mask, scaling, ridge, linking)


def rest_kernel(tile_of, count, core_ref, mask_ref, scaled_ref, *refs):
    lin_refs = refs[:count]
    send_ref, keep_ref, masked, buf = refs[count:]
    rows = scaled_ref.shape[0]
    devices, half = keep_ref.shape[1:3]
    unit = pl.program_id(0)
    for i in range(count):
        for t in range(rows // TILE):
            lanes = slice(t * TILE, (t + 1) * TILE)
            tile = lin_refs[i][lanes, :].astype(jnp.float32) * mask_ref[t, tile_of(unit, i)].astype(jnp.float32)
            masked[lanes, i * TILE : (i + 1) * TILE] = tile.astype(jnp.bfloat16)
    buf[...] = dot_rows(masked[...], scaled_ref[...])
    core = core_ref[0]
    for i in range(devices):
        base = 2 * half * i
        keep_ref[0, i] = buf[pl.ds(pl.multiple_of(base + core * half, half), half), :]
        send_ref[0, i] = buf[pl.ds(pl.multiple_of(base + (1 - core) * half, half), half), :]


def rest_products(core, tile_mask, scaled, linking, devices, units, tile_of):
    rows, width = scaled.shape
    count = (linking.shape[1] - width) // TILE // units
    half = count * TILE // devices // 2
    out = jax.ShapeDtypeStruct((units, devices, half, width), jnp.float32)
    return pl.pallas_call(
        functools.partial(rest_kernel, tile_of, count),
        grid=(units,),
        out_shape=(out, out),
        in_specs=[SMEM, SMEM, VMEM]
        + [pl.BlockSpec((rows, TILE), functools.partial(lambda i, g: (0, tile_of(g, i)), i)) for i in range(count)],
        out_specs=(pl.BlockSpec((1, devices, half, width), lambda g: (g, 0, 0, 0)),) * 2,
        scratch_shapes=[
            pltpu.VMEM((rows, count * TILE), jnp.bfloat16),
            pltpu.VMEM((count * TILE, width), jnp.float32),
        ],
        compiler_params=PARAMS,
        name="rest_products",
    )(core, tile_mask, scaled, *([linking] * count))


def factor_tile(block):
    groups = TILE // SUB
    sub = lax.broadcasted_iota(jnp.int32, (SUB, TILE), 0)
    lane = lax.broadcasted_iota(jnp.int32, (SUB, TILE), 1)
    left = [block[SUB * g : SUB * (g + 1), :] for g in range(groups)]
    right = [jnp.where(lane == sub + SUB * g, 1.0, 0.0).astype(jnp.float32) for g in range(groups)]
    upper, inverse = [], []

    def column(x, at):
        return jnp.broadcast_to(x[:, at : at + 1], (SUB, TILE))

    def row(x, at):
        return jnp.broadcast_to(x[at : at + 1, :], (SUB, TILE))

    for g in range(groups):
        a, q = left[g], right[g]
        cols = [column(a, SUB * g + k) for k in range(SUB)]
        recips, a_rows, q_rows, c_rows = [], [], [], []
        for j in range(SUB):
            recips.append(1.0 / row(cols[j], j))
            a_rows.append(row(a, j))
            q_rows.append(row(q, j))
            c_rows.append([row(cols[k], j) for k in range(SUB)])
            mult = jnp.where(sub > j, cols[j] * recips[j], 0.0)
            a = a - mult * a_rows[j]
            q = q - mult * q_rows[j]
            for k in range(j + 1, SUB):
                cols[k] = cols[k] - mult * c_rows[j][k]
        pivots = cols[0]
        for j in range(1, SUB):
            pivots = jnp.where(sub == j, cols[j], pivots)
        root = lax.rsqrt(pivots)
        upper.append(jnp.where(lane >= sub + SUB * g, a * root, 0.0))
        inverse.append(q * root)
        for m in range(g + 1, groups):
            a, q = left[m], right[m]
            cols = [column(a, SUB * g + k) for k in range(SUB)]
            for j in range(SUB):
                mult = cols[j] * recips[j]
                a = a - mult * a_rows[j]
                q = q - mult * q_rows[j]
                for k in range(j + 1, SUB):
                    cols[k] = cols[k] - mult * c_rows[j][k]
            left[m], right[m] = a, q
    return jnp.concatenate(upper, 0), jnp.concatenate(inverse, 0)


def factor_kernel(k, blocks, pieces, *refs):
    count = len(pieces)
    packed = refs[:count]
    uppers = refs[count : count + k]
    inverses = refs[count + k : count + 2 * k]
    upper_ref, inverse_ref, buf, sems = refs[count + 2 * k :]
    copies = []
    for n, (unit, begin, to, size) in enumerate(pieces):
        copies.append(
            pltpu.make_async_copy(packed[n].at[:, begin : begin + size], buf.at[:, to : to + size], sems.at[n])
        )
    for copy in copies:
        copy.start()
    for copy in copies:
        copy.wait()
    if k:
        total = buf[...]
        for j in range(k):
            at = (k - j) * TILE
            total = total - dot(uppers[j][:, at : at + TILE], uppers[j][:, at:], 0, 0)
        buf[...] = total
    upper, inverse = factor_tile(buf[:, :TILE])
    upper_ref[:, :TILE] = upper
    inverse_ref[:, k * TILE :] = inverse
    if k < blocks - 1:
        upper_ref[:, TILE:] = dot(inverse, buf[:, TILE:], 1, 0)
    for j in range(k):
        total = 0.0
        for l in range(j, k):
            at = (k - l) * TILE
            total = total + dot(uppers[l][:, at : at + TILE], inverses[l][:, j * TILE : (j + 1) * TILE], 0, 0)
        inverse_ref[:, j * TILE : (j + 1) * TILE] = -dot(inverse, total, 1, 0)


def factor_step(k, blocks, packed, uppers, inverses):
    begin = sum((blocks - j) * TILE for j in range(k))
    width = (blocks - k) * TILE
    pieces, start = [], 0
    for unit, piece in enumerate(packed):
        low, high = max(begin, start), min(begin + width, start + piece.shape[1])
        if low < high:
            pieces.append((unit, low - start, low - begin, high - low))
        start += piece.shape[1]
    return pl.pallas_call(
        functools.partial(factor_kernel, k, blocks, pieces),
        out_shape=(
            jax.ShapeDtypeStruct((TILE, width), jnp.float32),
            jax.ShapeDtypeStruct((TILE, (k + 1) * TILE), jnp.float32),
        ),
        in_specs=[ANY] * len(pieces) + [VMEM] * (2 * k),
        out_specs=(VMEM, VMEM),
        scratch_shapes=[pltpu.VMEM((TILE, width), jnp.float32), pltpu.SemaphoreType.DMA((len(pieces),))],
        compiler_params=PARAMS,
        name="factor_step",
    )(*[packed[p[0]] for p in pieces], *uppers, *inverses)


def tile_rows_kernel(blocks, at_ref, *refs):
    uppers, out_ref = refs[:blocks], refs[blocks]
    at = at_ref[0]
    for j in range(blocks):
        cols = slice(j * TILE, (j + 1) * TILE)

        @pl.when(at >= j)
        def _():
            lanes = pl.ds(pl.multiple_of((at - j) * TILE, TILE), TILE)
            out_ref[:, cols] = jnp.transpose(uppers[j][:, lanes])

        @pl.when(at < j)
        def _():
            out_ref[:, cols] = jnp.zeros((TILE, TILE), jnp.float32)


def tile_rows(at, uppers):
    blocks = len(uppers)
    return pl.pallas_call(
        functools.partial(tile_rows_kernel, blocks),
        out_shape=jax.ShapeDtypeStruct((TILE, blocks * TILE), jnp.float32),
        in_specs=[SMEM] + [VMEM] * blocks,
        out_specs=VMEM,
        compiler_params=PARAMS,
        name="tile_rows",
    )(at, *uppers)


def below_kernel(blocks, units, core_ref, *refs):
    mine, other = refs[:units], refs[units : 2 * units]
    inverses = refs[2 * units : 2 * units + blocks]
    out_ref, buf = refs[2 * units + blocks :]
    core = core_ref[0]
    half = mine[0].shape[0]
    for u in range(units):
        base = 2 * half * u
        buf[pl.ds(pl.multiple_of(base + core * half, 8), half), :] = mine[u][...]
        buf[pl.ds(pl.multiple_of(base + (1 - core) * half, 8), half), :] = other[u][...]
    for j in range(blocks):
        span = (j + 1) * TILE
        out_ref[:, j * TILE : span] = dot(buf[:, :span], inverses[j][...], 1, 1)


def below_rows(core, mine, other, inverses):
    units, blocks = len(mine), len(inverses)
    shape = (2 * units * mine[0].shape[0], mine[0].shape[1])
    return pl.pallas_call(
        functools.partial(below_kernel, blocks, units),
        out_shape=jax.ShapeDtypeStruct(shape, jnp.float32),
        in_specs=[SMEM] + [VMEM] * (2 * units + blocks),
        out_specs=VMEM,
        scratch_shapes=[pltpu.VMEM(shape, jnp.float32)],
        compiler_params=PARAMS,
        name="below_rows",
    )(core, *mine, *other, *inverses)


def swap_cores(x):
    return lax.ppermute(x, "period", [(0, 1), (1, 0)])


def swap_rows(x, bit):
    devices = lax.axis_size("row")
    return lax.ppermute(x, "row", [(r, r ^ (1 << bit)) for r in range(devices)])


def my_bit(bit):
    return lax.rem(lax.div(lax.axis_index("row"), 1 << bit), 2)


def halve(mine, other, order):
    left = sorted(order, reverse=True)
    for bit in order:
        axis = left.index(bit)
        left.remove(bit)
        here = my_bit(bit)

        def part(which):
            return lax.dynamic_index_in_dim(mine, which, axis, keepdims=False) + lax.dynamic_index_in_dim(
                other, which, axis, keepdims=False
            )

        received = swap_rows(part(1 - here), bit)
        mine, other = part(here), received
    return mine + other


def join(mine, other, here, axis):
    return jnp.where(here == 0, jnp.stack([mine, other], axis), jnp.stack([other, mine], axis))


def double(piece, order):
    have = []
    for bit in reversed(order):
        have = sorted(have + [bit], reverse=True)
        piece = join(piece, swap_rows(piece, bit), my_bit(bit), have.index(bit))
    return piece


def shards(linking, tile_mask, scaling, link_diag):
    row_devs = lax.axis_size("row")
    bits = row_devs.bit_length() - 1
    diag_rows = link_diag.shape[0]
    panel = diag_rows * row_devs
    blocks = panel // TILE
    rest_rows = (linking.shape[1] - panel) // row_devs
    row_index = lax.axis_index("row")
    core = lax.axis_index("period")
    core_arg = core.astype(jnp.int32).reshape(1)

    first = jnp.where(core == 0, link_diag, 0.0)
    ridge = lax.dynamic_update_slice(jnp.zeros((panel,), jnp.float32), first, (row_index * diag_rows,))
    diag_send, diag_keep, scaled = diag_products(
        core_arg, tile_mask, scaling.reshape(-1, TILE), ridge.reshape(blocks, TILE), linking, panel
    )
    near, far = list(range(bits)), [1, 0] + list(range(2, bits))

    lead = (2,) * bits + (-1,)
    diag_got = swap_cores(diag_send)
    packed = []
    cut = diag_keep.shape[1] // 2
    for unit, order in enumerate((near, far)):
        lanes = slice(unit * cut, (unit + 1) * cut)
        piece = halve(diag_keep[:, lanes].reshape(lead + (cut,)), diag_got[:, lanes].reshape(lead + (cut,)), order)
        piece = double(piece, order)
        packed.append(join(piece, swap_cores(piece), core, 0).reshape(TILE, cut))

    per_dev = rest_rows // TILE
    if rest_rows % TILE == 0:
        units = per_dev
        tile_of = lambda unit, i: blocks + i * per_dev + unit
    else:
        units = 1
        tile_of = lambda unit, i: blocks + i
    rest_send, rest_keep = rest_products(core_arg, tile_mask, scaled, linking, row_devs, units, tile_of)
    rest_got = swap_cores(rest_send)
    mine, other = [], []
    for unit in range(units):
        shape = (2,) * bits + (rest_rows // units // 2, panel)
        order = near if unit < 2 else far
        piece = halve(rest_keep[unit].reshape(shape), rest_got[unit].reshape(shape), order)
        mine.append(piece)
        other.append(swap_cores(piece))

    uppers, inverses = [], []
    for k in range(blocks):
        upper, inverse = factor_step(k, blocks, packed, uppers, inverses)
        uppers.append(upper)
        inverses.append(inverse)
    at = row_index * diag_rows
    rows = tile_rows((at // TILE).astype(jnp.int32).reshape(1), uppers)
    my_factor = lax.dynamic_slice_in_dim(rows, at % TILE, diag_rows, 0)
    below = below_rows(core_arg, mine, other, inverses)
    return my_factor, below


def solution(mesh):
    whole = P(("inst", "period", "row"), None)
    out = P(("inst", "row"), None)
    return jax.shard_map(
        shards,
        mesh=mesh,
        in_specs=(whole, whole, P(("inst", "period", "row")), P(("inst", "row"))),
        out_specs=(out, out),
        check_vma=False,
    )
```

```python
import functools

import jax
import jax.numpy as jnp
from jax import lax
from jax.experimental import pallas as pl
from jax.experimental.pallas import tpu as pltpu
from jax.sharding import PartitionSpec as P

TILE = 128
SUB = 8
HIGH = lax.Precision.HIGHEST
VMEM = pl.BlockSpec(memory_space=pltpu.VMEM)
SMEM = pl.BlockSpec(memory_space=pltpu.SMEM)
ANY = pl.BlockSpec(memory_space=pl.ANY)
WIDTHS = (256, 384, 384)
PLAN = {"s1": [0], "f": [1], "f0": [0], "f1": [2], "f2": [1], "f3": [0], "f4": [1, 2], "f5": [2, 0], "end": [1, 2]}
PARAMS = pltpu.CompilerParams(vmem_limit_bytes=48 << 20)


def cost(us):
    return pl.CostEstimate(flops=int(us * 1.1e9), bytes_accessed=int(us * 3.5e6), transcendentals=0)


def dot(a, b, contract_a, contract_b):
    return lax.dot_general(
        a, b, (((contract_a,), (contract_b,)), ((), ())), precision=HIGH, preferred_element_type=jnp.float32
    )


def dot_rows(a, b):
    return lax.dot_general(a, b, (((0,), (0,)), ((), ())), preferred_element_type=jnp.float32)


def dot_cols(a, b):
    return lax.dot_general(a, b, (((1,), (1,)), ((), ())), preferred_element_type=jnp.float32)


def split(x):
    high = x.astype(jnp.bfloat16)
    return high, (x - high.astype(jnp.float32)).astype(jnp.bfloat16)


def dot_three(a, b):
    (a_high, a_low), (b_high, b_low) = split(a), split(b)

    def one(x, y):
        return jnp.dot(x, y, preferred_element_type=jnp.float32)

    return one(a_low, b_high) + one(a_high, b_low) + one(a_high, b_high)


def crossed_row(index, devices):
    if devices < 4:
        return index
    return index // 4 * 4 + index % 2 * 2 + index // 2 % 2


def diag_kernel(core_ref, mask_ref, scale_ref, ridge_ref, lin_ref, send_ref, keep_ref, scaled_ref, masked, buf):
    rows, width = lin_ref.shape
    blocks = width // TILE
    half = TILE // 2
    for t in range(rows // TILE):
        lanes = slice(t * TILE, (t + 1) * TILE)
        factor = jnp.transpose(jnp.broadcast_to(scale_ref[t : t + 1, :], (TILE, TILE)))
        for i in range(blocks):
            cols = slice(i * TILE, (i + 1) * TILE)
            tile = lin_ref[lanes, cols].astype(jnp.float32) * mask_ref[t, i].astype(jnp.float32)
            masked[lanes, cols] = tile.astype(jnp.bfloat16)
            scaled_ref[lanes, cols] = (factor * tile).astype(jnp.bfloat16)
    eye = lax.broadcasted_iota(jnp.int32, (TILE, TILE), 0) == lax.broadcasted_iota(jnp.int32, (TILE, TILE), 1)
    start = 0
    for j in range(blocks):
        first = slice(j * TILE, (j + 1) * TILE)
        span = (blocks - j) * TILE
        buf[:, start : start + span] = 0.5 * (
            dot_rows(scaled_ref[:, first], masked[:, j * TILE :]) + dot_rows(masked[:, first], scaled_ref[:, j * TILE :])
        )
        buf[:, start : start + TILE] += jnp.where(eye, ridge_ref[j : j + 1, :], 0.0)
        start += span
    core = core_ref[0]
    keep_ref[...] = buf[pl.ds(pl.multiple_of(core * half, half), half), :]
    send_ref[...] = buf[pl.ds(pl.multiple_of((1 - core) * half, half), half), :]


def diag_products(core, tile_mask, scaling, ridge, linking, width):
    rows = linking.shape[0]
    blocks = width // TILE
    packed = blocks * (blocks + 1) // 2 * TILE
    half = jax.ShapeDtypeStruct((TILE // 2, packed), jnp.float32)
    return pl.pallas_call(
        diag_kernel,
        grid=(1,),
        out_shape=(half, half, jax.ShapeDtypeStruct((rows, width), jnp.bfloat16)),
        in_specs=[SMEM, SMEM, VMEM, VMEM, pl.BlockSpec((rows, width), lambda g: (0, 0))],
        out_specs=(VMEM, VMEM, VMEM),
        scratch_shapes=[pltpu.VMEM((rows, width), jnp.bfloat16), pltpu.VMEM((TILE, packed), jnp.float32)],
        compiler_params=PARAMS,
        cost_estimate=cost(5),
        name="diag_products",
    )(core, tile_mask, scaling, ridge, linking)


def rest_kernel(first, spans, count, core_ref, mask_ref, scaled_ref, *refs):
    lin_refs = refs[:count]
    out_refs = refs[count : count + 2 * len(spans)]
    masked, buf = refs[count + 2 * len(spans) :]
    rows, width = lin_refs[0].shape
    devices, half = out_refs[0].shape[:2]
    for n in range(count):
        for i in range(width // TILE):
            cols = slice(i * TILE, (i + 1) * TILE)
            to = slice(n * width + i * TILE, n * width + (i + 1) * TILE)
            for t in range(rows // TILE):
                down = slice(t * TILE, (t + 1) * TILE)
                flag = mask_ref[t, first + n * (width // TILE) + i].astype(jnp.float32)
                masked[down, to] = (lin_refs[n][down, cols].astype(jnp.float32) * flag).astype(jnp.bfloat16)
    start = spans[0].start
    buf[...] = dot_rows(masked[...], scaled_ref[:, start : spans[-1].stop])
    core = core_ref[0]
    for n, span in enumerate(spans):
        lanes = slice(span.start - start, span.stop - start)
        for i in range(devices):
            straight, crossed = 2 * half * i, 2 * half * crossed_row(i, devices)
            send = jnp.where(core == 0, crossed + half, straight)
            keep = jnp.where(core == 0, straight, crossed + half)
            out_refs[2 * n][i] = buf[pl.ds(pl.multiple_of(send, half), half), lanes]
            out_refs[2 * n + 1][i] = buf[pl.ds(pl.multiple_of(keep, half), half), lanes]


def rest_products(core, tile_mask, scaled, linking, devices, spans):
    rows, panel = scaled.shape
    below = linking.shape[1] - panel
    count = below // panel
    half = below // devices // 2
    outs = [jax.ShapeDtypeStruct((devices, half, span.stop - span.start), jnp.float32) for span in spans for _ in range(2)]
    return pl.pallas_call(
        functools.partial(rest_kernel, panel // TILE, spans, count),
        grid=(1,),
        out_shape=outs,
        in_specs=[SMEM, SMEM, VMEM]
        + [pl.BlockSpec((rows, panel), functools.partial(lambda n, g: (0, n + 1), n)) for n in range(count)],
        out_specs=[VMEM] * len(outs),
        scratch_shapes=[
            pltpu.VMEM((rows, below), jnp.bfloat16),
            pltpu.VMEM((below, spans[-1].stop - spans[0].start), jnp.float32),
        ],
        compiler_params=PARAMS,
        cost_estimate=cost(6),
        name="rest_products",
    )(core, tile_mask, scaled, *([linking] * count))


def factor_tile(block):
    groups, per_half = TILE // SUB, TILE // SUB // 2
    sub = lax.broadcasted_iota(jnp.int32, (SUB, TILE), 0)
    lane = lax.broadcasted_iota(jnp.int32, (SUB, TILE), 1)

    def column(x, at):
        return jnp.broadcast_to(x[:, at : at + 1], (SUB, TILE))

    def row(x, at):
        return jnp.broadcast_to(x[at : at + 1, :], (SUB, TILE))

    left = [block[SUB * g : SUB * (g + 1), :] for g in range(groups)]
    right = [jnp.where(lane == sub + SUB * g, 1.0, 0.0).astype(jnp.float32) for g in range(groups)]
    upper, inverse = [], []
    for g in range(groups):
        if g == per_half:
            both = jnp.concatenate([jnp.concatenate(upper, 0), jnp.concatenate(inverse, 0)], 1)
            later = jnp.transpose(both[:, :TILE])[SUB * g :, :]
            update = dot(later, both, 1, 0)
            for m in range(g, groups):
                at = slice(SUB * (m - g), SUB * (m - g + 1))
                left[m], right[m] = left[m] - update[at, :TILE], right[m] - update[at, TILE:]
        a, q = left[g], right[g]
        cols = [column(a, SUB * g + k) for k in range(SUB)]
        recips, a_rows, q_rows, c_rows = [], [], [], []
        for j in range(SUB):
            if j % 2 == 0:
                pivot, beside, below = row(cols[j], j), row(cols[j + 1], j), row(cols[j + 1], j + 1)
                recips += [1.0 / pivot, pivot * (1.0 / (pivot * below - beside * beside))]
            a_rows.append(row(a, j))
            q_rows.append(row(q, j))
            c_rows.append([row(cols[k], j) for k in range(SUB)])
            mult = jnp.where(sub > j, cols[j], 0.0) * recips[j]
            a = a - mult * a_rows[j]
            q = q - mult * q_rows[j]
            for k in range(j + 1, SUB):
                cols[k] = cols[k] - mult * c_rows[j][k]
        pivots = cols[0]
        for j in range(1, SUB):
            pivots = jnp.where(sub == j, cols[j], pivots)
        root = lax.rsqrt(pivots)
        upper.append(jnp.where(lane >= sub + SUB * g, a * root, 0.0))
        inverse.append(q * root)
        for m in range(g + 1, per_half if g < per_half else groups):
            a, q = left[m], right[m]
            cols = [column(a, SUB * g + k) for k in range(SUB)]
            for j in range(SUB):
                mult = cols[j] * recips[j]
                a = a - mult * a_rows[j]
                q = q - mult * q_rows[j]
                for k in range(j + 1, SUB):
                    cols[k] = cols[k] - mult * c_rows[j][k]
            left[m], right[m] = a, q
    return jnp.concatenate(upper, 0), jnp.concatenate(inverse, 0)


def unpack_kernel(blocks, core_ref, mine_ref, other_ref, packed_ref, upper_ref, inverse_ref, sems):
    half, first = TILE // 2, blocks * TILE
    core = core_ref[0]
    copies = []
    for lanes in (slice(0, first), slice(first, packed_ref.shape[1])):
        for ref, which in ((mine_ref, core), (other_ref, 1 - core)):
            rows = pl.ds(pl.multiple_of(which * half, half), half)
            copies.append(pltpu.make_async_copy(ref.at[:, lanes], packed_ref.at[rows, lanes], sems.at[len(copies)]))
    for copy in copies:
        copy.start()
    copies[0].wait()
    copies[1].wait()
    upper, inverse = factor_tile(packed_ref[:, :TILE])
    upper_ref[:, :TILE] = upper
    inverse_ref[...] = inverse
    upper_ref[:, TILE:] = dot(inverse, packed_ref[:, TILE:first], 1, 0)
    copies[2].wait()
    copies[3].wait()


def unpack_step(blocks, core, mine, other):
    return pl.pallas_call(
        functools.partial(unpack_kernel, blocks),
        out_shape=(
            jax.ShapeDtypeStruct((TILE, mine.shape[1]), jnp.float32),
            jax.ShapeDtypeStruct((TILE, blocks * TILE), jnp.float32),
            jax.ShapeDtypeStruct((TILE, TILE), jnp.float32),
        ),
        in_specs=[SMEM, ANY, ANY],
        out_specs=(VMEM, VMEM, VMEM),
        scratch_shapes=[pltpu.SemaphoreType.DMA((4,))],
        compiler_params=PARAMS,
        cost_estimate=cost(5),
        name="unpack_step",
    )(core, mine, other)


def factor_kernel(k, blocks, begin, packed_ref, *refs):
    uppers, inverses = refs[:k], refs[k : 2 * k]
    upper_ref, inverse_ref, buf, sem = refs[2 * k :]
    copy = pltpu.make_async_copy(packed_ref.at[:, begin : begin + buf.shape[1]], buf, sem)
    copy.start()
    turned = [jnp.transpose(uppers[j][:, (k - j) * TILE : (k - j + 1) * TILE]) for j in range(k)]
    copy.wait()
    if k:
        total = buf[...]
        for j in range(k):
            total = total - dot(turned[j], uppers[j][:, (k - j) * TILE :], 1, 0)
        buf[...] = total
    upper, inverse = factor_tile(buf[:, :TILE])
    upper_ref[:, :TILE] = upper
    inverse_ref[:, k * TILE :] = inverse
    if k < blocks - 1:
        upper_ref[:, TILE:] = dot(inverse, buf[:, TILE:], 1, 0)
    if k:
        inverse_ref[:, : k * TILE] = jnp.zeros((TILE, k * TILE), jnp.float32)
        for j in range(k):
            inverse_ref[:, : (j + 1) * TILE] += dot_three(turned[j], inverses[j][...])
        inverse_ref[:, : k * TILE] = -dot_three(inverse, inverse_ref[:, : k * TILE])


def factor_step(k, blocks, packed, uppers, inverses):
    begin = sum((blocks - j) * TILE for j in range(k))
    width = (blocks - k) * TILE
    return pl.pallas_call(
        functools.partial(factor_kernel, k, blocks, begin),
        out_shape=(
            jax.ShapeDtypeStruct((TILE, width), jnp.float32),
            jax.ShapeDtypeStruct((TILE, (k + 1) * TILE), jnp.float32),
        ),
        in_specs=[ANY] + [VMEM] * (2 * k),
        out_specs=(VMEM, VMEM),
        scratch_shapes=[pltpu.VMEM((TILE, width), jnp.float32), pltpu.SemaphoreType.DMA],
        compiler_params=PARAMS,
        cost_estimate=cost(7),
        name="factor_step",
    )(packed, *uppers, *inverses)


def tile_rows_kernel(blocks, at_ref, *refs):
    uppers, out_ref = refs[:blocks], refs[blocks]
    at = at_ref[0]
    for j in range(blocks):
        cols = slice(j * TILE, (j + 1) * TILE)

        @pl.when(at >= j)
        def _():
            lanes = pl.ds(pl.multiple_of((at - j) * TILE, TILE), TILE)
            out_ref[:, cols] = jnp.transpose(uppers[j][:, lanes])

        @pl.when(at < j)
        def _():
            out_ref[:, cols] = jnp.zeros((TILE, TILE), jnp.float32)


def tile_rows(at, uppers):
    blocks = len(uppers)
    return pl.pallas_call(
        functools.partial(tile_rows_kernel, blocks),
        out_shape=jax.ShapeDtypeStruct((TILE, blocks * TILE), jnp.float32),
        in_specs=[SMEM] + [VMEM] * blocks,
        out_specs=VMEM,
        compiler_params=PARAMS,
        cost_estimate=cost(1.5),
        name="tile_rows",
    )(at, *uppers)


def below_kernel(blocks, units, core_ref, *refs):
    mine, other = refs[:units], refs[units : 2 * units]
    inverses = refs[2 * units : 2 * units + blocks]
    out_ref, buf = refs[2 * units + blocks :]
    core = core_ref[0]
    half, start = mine[0].shape[0], 0
    for u in range(units):
        lanes = slice(start, start + mine[u].shape[1])
        buf[pl.ds(pl.multiple_of(core * half, 8), half), lanes] = mine[u][...]
        buf[pl.ds(pl.multiple_of((1 - core) * half, 8), half), lanes] = other[u][...]
        start = lanes.stop
    high, low = split(buf[...])
    for j in range(blocks):
        span = (j + 1) * TILE
        inv_high, inv_low = split(inverses[j][...])
        total = dot_cols(low[:, :span], inv_high) + dot_cols(high[:, :span], inv_low)
        out_ref[:, j * TILE : span] = total + dot_cols(high[:, :span], inv_high)


def below_rows(core, mine, other, inverses):
    units, blocks = len(mine), len(inverses)
    shape = (2 * mine[0].shape[0], blocks * TILE)
    return pl.pallas_call(
        functools.partial(below_kernel, blocks, units),
        out_shape=jax.ShapeDtypeStruct(shape, jnp.float32),
        in_specs=[SMEM] + [VMEM] * (2 * units + blocks),
        out_specs=VMEM,
        scratch_shapes=[pltpu.VMEM(shape, jnp.float32)],
        compiler_params=PARAMS,
        cost_estimate=cost(4),
        name="below_rows",
    )(core, *mine, *other, *inverses)


def after(x, *others):
    return lax.optimization_barrier((x, others))[0] if others else x


def swap_cores(x):
    return lax.ppermute(x, "period", [(0, 1), (1, 0)])


def place():
    row, devices = lax.axis_index("row"), lax.axis_size("row")
    if devices < 4:
        return row
    crossed = lax.div(row, 4) * 4 + lax.rem(row, 2) * 2 + lax.rem(lax.div(row, 2), 2)
    return jnp.where(lax.axis_index("period") == 0, row, crossed)


def swap_places(x, bit):
    devices = lax.axis_size("row")
    pairs = []
    for row in range(devices):
        pairs.append((row, row ^ (1 << bit)))
        crossed = crossed_row(crossed_row(row, devices) ^ (1 << bit), devices)
        pairs.append((devices + row, devices + crossed))
    return lax.ppermute(x, ("period", "row"), pairs)


def my_bit(bit):
    return lax.rem(lax.div(place(), 1 << bit), 2)


def part(x, dims, chosen):
    starts = [chosen.get(bit, 0) for bit in dims] + [0] * (x.ndim - len(dims))
    sizes = [1 if bit in chosen else 2 for bit in dims] + list(x.shape[len(dims) :])
    out = lax.dynamic_slice(x, starts, sizes)
    return out.reshape([2] * sum(bit not in chosen for bit in dims) + list(x.shape[len(dims) :]))


class Halving:
    def __init__(self, mine, other, bits):
        dims = list(reversed(range(bits)))
        self.terms = [(mine, dims), (other, dims)]
        self.chosen = {}
        self.bit = 0

    def total(self, chosen, *deps):
        self.terms[-1] = (after(self.terms[-1][0], *deps), self.terms[-1][1])
        return sum(part(x, dims, {b: v for b, v in chosen.items() if b in dims}) for x, dims in self.terms)

    def send(self, *deps):
        here = my_bit(self.bit)
        sent = self.total({**self.chosen, self.bit: 1 - here}, *deps)
        self.chosen[self.bit] = here
        dims = [b for b in self.terms[0][1] if b not in self.chosen]
        self.terms.append((swap_places(sent, self.bit), dims))
        self.bit += 1
        return sent

    def result(self, *deps):
        return self.total(self.chosen, *deps)


def join(mine, other, here, axis):
    return jnp.where(here == 0, jnp.stack([mine, other], axis), jnp.stack([other, mine], axis))


def shards(linking, tile_mask, scaling, link_diag):
    row_devs = lax.axis_size("row")
    bits = row_devs.bit_length() - 1
    diag_rows = link_diag.shape[0]
    panel = diag_rows * row_devs
    blocks = panel // TILE
    rest_rows = (linking.shape[1] - panel) // row_devs
    row_index = lax.axis_index("row")
    core = lax.axis_index("period")
    core_arg = core.astype(jnp.int32).reshape(1)

    first = jnp.where(core == 0, link_diag, 0.0)
    ridge = lax.dynamic_update_slice(jnp.zeros((panel,), jnp.float32), first, (row_index * diag_rows,))
    diag_send, diag_keep, scaled = diag_products(
        core_arg, tile_mask, scaling.reshape(-1, TILE), ridge.reshape(blocks, TILE), linking, panel
    )
    diag_got = swap_cores(diag_send)

    units = len(WIDTHS)
    unit_lead = (2,) * bits + (rest_rows // 2,)
    rest, made = [], []

    def make_units(first, last, *deps):
        starts = [sum(WIDTHS[:u]) for u in range(units + 1)]
        spans = [slice(starts[u], starts[u + 1]) for u in range(first, last)]
        outs = rest_products(core_arg, tile_mask, after(scaled, *deps), linking, row_devs, spans)
        made.append(outs[0])
        for u in range(first, last):
            send, keep = outs[2 * (u - first)], outs[2 * (u - first) + 1]
            shape = unit_lead + (WIDTHS[u],)
            rest.append(Halving(keep.reshape(shape), swap_cores(send).reshape(shape), bits))

    plan = PLAN if bits == 3 else {"f0": [u for u in range(units) for _ in range(bits)], "end": list(range(units))}
    results = {}

    def more(stage, gate):
        sent = []
        for u in plan.get(stage, []):
            if rest[u].bit < bits:
                sent.append(rest[u].send(*gate))
            else:
                mine = rest[u].result(*gate)
                results[u] = (mine, swap_cores(mine))
                sent.append(mine)
        return sent

    lead = (2,) * bits + (-1, diag_keep.shape[1])
    diag = Halving(diag_keep.reshape(lead), diag_got.reshape(lead), bits)
    gate = []
    for step in range(bits - 1):
        sent = diag.send(*gate)
        if step == 0:
            make_units(0, 1, sent)
        gate = made[-1:] + more(f"s{step}", [sent])
    piece = after(diag.result(), *gate)
    got = swap_places(piece, bits - 1)
    early = [r.terms[-1][0] for r in rest if r.bit]
    make_units(1, units, piece)
    gate = made[-1:] + more("x", [piece])
    piece = piece + after(got, *gate)
    for step in reversed(range(bits - 1)):
        piece = after(piece, *gate)
        if step == 0:
            piece = after(piece, *early)
        gate = more(f"d{step}", [piece])
        piece = join(piece, swap_places(piece, step), my_bit(step), bits - 1 - step)
    half = after(piece.reshape(diag_keep.shape), *gate)
    packed = (half, swap_cores(half))

    uppers, inverses = [], []
    gate = more("f", [half])
    for k in range(blocks):
        inputs = after((packed, uppers, inverses), *gate)
        if k == 0:
            packed, upper, inverse = unpack_step(blocks, core_arg, *inputs[0])
        else:
            upper, inverse = factor_step(k, blocks, *inputs)
        uppers.append(upper)
        inverses.append(inverse)
        gate = more(f"f{k}", [upper])
    at = row_index * diag_rows
    rows = tile_rows((at // TILE).astype(jnp.int32).reshape(1), uppers)
    my_factor = lax.dynamic_slice_in_dim(rows, at % TILE, diag_rows, 0)
    more("end", [rows])
    mine, other = zip(*[results[u] for u in range(units)])
    below = below_rows(core_arg, mine, other, inverses)
    return my_factor, below


def solution(mesh):
    whole = P(("inst", "period", "row"), None)
    out = P(("inst", "row"), None)
    return jax.shard_map(
        shards,
        mesh=mesh,
        in_specs=(whole, whole, P(("inst", "period", "row")), P(("inst", "row"))),
        out_specs=(out, out),
        check_vma=False,
    )
```

```python
import functools

import jax
import jax.numpy as jnp
from jax import lax
from jax.experimental import pallas as pl
from jax.experimental.pallas import tpu as pltpu
from jax.sharding import PartitionSpec as P

TILE = 128
SUB = 8
HIGH = lax.Precision.HIGHEST
VMEM = pl.BlockSpec(memory_space=pltpu.VMEM)
SMEM = pl.BlockSpec(memory_space=pltpu.SMEM)
ANY = pl.BlockSpec(memory_space=pl.ANY)
WIDTHS = (256, 384, 384)
PLAN = {"x": [0], "f": [1], "f0": [0], "f1": [2], "f2": [1], "f3": [0], "f4": [2, 1], "f5": [2, 0], "end": [1, 2]}
PARAMS = pltpu.CompilerParams(vmem_limit_bytes=48 << 20)


def cost(us):
    return pl.CostEstimate(flops=int(us * 1.1e9), bytes_accessed=int(us * 3.5e6), transcendentals=0)


def dot(a, b, contract_a, contract_b):
    return lax.dot_general(
        a, b, (((contract_a,), (contract_b,)), ((), ())), precision=HIGH, preferred_element_type=jnp.float32
    )


def dot_rows(a, b):
    return lax.dot_general(a, b, (((0,), (0,)), ((), ())), preferred_element_type=jnp.float32)


def dot_cols(a, b):
    return lax.dot_general(a, b, (((1,), (1,)), ((), ())), preferred_element_type=jnp.float32)


def split(x):
    high = x.astype(jnp.bfloat16)
    return high, (x - high.astype(jnp.float32)).astype(jnp.bfloat16)


def dot_three(a, b):
    (a_high, a_low), (b_high, b_low) = split(a), split(b)

    def one(x, y):
        return jnp.dot(x, y, preferred_element_type=jnp.float32)

    return one(a_low, b_high) + one(a_high, b_low) + one(a_high, b_high)


def crossed_row(index, devices):
    if devices < 4:
        return index
    return index // 4 * 4 + index % 2 * 2 + index // 2 % 2


def diag_kernel(core_ref, mask_ref, scale_ref, ridge_ref, lin_ref, send_ref, keep_ref, scaled_ref, masked, buf):
    rows, width = lin_ref.shape
    blocks = width // TILE
    half = TILE // 2
    for t in range(rows // TILE):
        lanes = slice(t * TILE, (t + 1) * TILE)
        factor = jnp.transpose(jnp.broadcast_to(scale_ref[t : t + 1, :], (TILE, TILE)))
        for i in range(blocks):
            cols = slice(i * TILE, (i + 1) * TILE)
            tile = lin_ref[lanes, cols].astype(jnp.float32) * mask_ref[t, i].astype(jnp.float32)
            masked[lanes, cols] = tile.astype(jnp.bfloat16)
            scaled_ref[lanes, cols] = (factor * tile).astype(jnp.bfloat16)
    eye = lax.broadcasted_iota(jnp.int32, (TILE, TILE), 0) == lax.broadcasted_iota(jnp.int32, (TILE, TILE), 1)
    start = 0
    for j in range(blocks):
        first = slice(j * TILE, (j + 1) * TILE)
        span = (blocks - j) * TILE
        buf[:, start : start + span] = 0.5 * (
            dot_rows(scaled_ref[:, first], masked[:, j * TILE :]) + dot_rows(masked[:, first], scaled_ref[:, j * TILE :])
        )
        buf[:, start : start + TILE] += jnp.where(eye, ridge_ref[j : j + 1, :], 0.0)
        start += span
    core = core_ref[0]
    keep_ref[...] = buf[pl.ds(pl.multiple_of(core * half, half), half), :]
    send_ref[...] = buf[pl.ds(pl.multiple_of((1 - core) * half, half), half), :]


def diag_products(core, tile_mask, scaling, ridge, linking, width):
    rows = linking.shape[0]
    blocks = width // TILE
    packed = blocks * (blocks + 1) // 2 * TILE
    half = jax.ShapeDtypeStruct((TILE // 2, packed), jnp.float32)
    return pl.pallas_call(
        diag_kernel,
        grid=(1,),
        out_shape=(half, half, jax.ShapeDtypeStruct((rows, width), jnp.bfloat16)),
        in_specs=[SMEM, SMEM, VMEM, VMEM, pl.BlockSpec((rows, width), lambda g: (0, 0))],
        out_specs=(VMEM, VMEM, VMEM),
        scratch_shapes=[pltpu.VMEM((rows, width), jnp.bfloat16), pltpu.VMEM((TILE, packed), jnp.float32)],
        compiler_params=PARAMS,
        cost_estimate=cost(5),
        name="diag_products",
    )(core, tile_mask, scaling, ridge, linking)


def rest_kernel(first, spans, count, core_ref, mask_ref, scaled_ref, *refs):
    lin_refs = refs[:count]
    out_refs = refs[count : count + 2 * len(spans)]
    masked, buf = refs[count + 2 * len(spans) :]
    rows, width = lin_refs[0].shape
    devices, half = out_refs[0].shape[:2]
    for n in range(count):
        for i in range(width // TILE):
            cols = slice(i * TILE, (i + 1) * TILE)
            to = slice(n * width + i * TILE, n * width + (i + 1) * TILE)
            for t in range(rows // TILE):
                down = slice(t * TILE, (t + 1) * TILE)
                flag = mask_ref[t, first + n * (width // TILE) + i].astype(jnp.float32)
                masked[down, to] = (lin_refs[n][down, cols].astype(jnp.float32) * flag).astype(jnp.bfloat16)
    start = spans[0].start
    buf[...] = dot_rows(masked[...], scaled_ref[:, start : spans[-1].stop])
    core = core_ref[0]
    for n, span in enumerate(spans):
        lanes = slice(span.start - start, span.stop - start)
        for i in range(devices):
            straight, crossed = 2 * half * i, 2 * half * crossed_row(i, devices)
            send = jnp.where(core == 0, crossed + half, straight)
            keep = jnp.where(core == 0, straight, crossed + half)
            out_refs[2 * n][i] = buf[pl.ds(pl.multiple_of(send, half), half), lanes]
            out_refs[2 * n + 1][i] = buf[pl.ds(pl.multiple_of(keep, half), half), lanes]


def rest_products(core, tile_mask, scaled, linking, devices, spans):
    rows, panel = scaled.shape
    below = linking.shape[1] - panel
    count = below // panel
    half = below // devices // 2
    outs = [jax.ShapeDtypeStruct((devices, half, span.stop - span.start), jnp.float32) for span in spans for _ in range(2)]
    return pl.pallas_call(
        functools.partial(rest_kernel, panel // TILE, spans, count),
        grid=(1,),
        out_shape=outs,
        in_specs=[SMEM, SMEM, VMEM]
        + [pl.BlockSpec((rows, panel), functools.partial(lambda n, g: (0, n + 1), n)) for n in range(count)],
        out_specs=[VMEM] * len(outs),
        scratch_shapes=[
            pltpu.VMEM((rows, below), jnp.bfloat16),
            pltpu.VMEM((below, spans[-1].stop - spans[0].start), jnp.float32),
        ],
        compiler_params=PARAMS,
        cost_estimate=cost(6),
        name="rest_products",
    )(core, tile_mask, scaled, *([linking] * count))


def factor_tile(block):
    groups, per_half = TILE // SUB, TILE // SUB // 2
    sub = lax.broadcasted_iota(jnp.int32, (SUB, TILE), 0)
    lane = lax.broadcasted_iota(jnp.int32, (SUB, TILE), 1)

    def column(x, at):
        return jnp.broadcast_to(x[:, at : at + 1], (SUB, TILE))

    def row(x, at):
        return jnp.broadcast_to(x[at : at + 1, :], (SUB, TILE))

    left = [block[SUB * g : SUB * (g + 1), :] for g in range(groups)]
    right = [jnp.where(lane == sub + SUB * g, 1.0, 0.0).astype(jnp.float32) for g in range(groups)]
    upper, inverse = [], []
    for g in range(groups):
        if g == per_half:
            both = jnp.concatenate([jnp.concatenate(upper, 0), jnp.concatenate(inverse, 0)], 1)
            later = jnp.transpose(both[:, :TILE])[SUB * g :, :]
            update = dot(later, both, 1, 0)
            for m in range(g, groups):
                at = slice(SUB * (m - g), SUB * (m - g + 1))
                left[m], right[m] = left[m] - update[at, :TILE], right[m] - update[at, TILE:]
        a, q = left[g], right[g]
        cols = [column(a, SUB * g + k) for k in range(SUB)]
        recips, a_rows, q_rows, c_rows = [], [], [], []
        for j in range(SUB):
            if j % 2 == 0:
                pivot, beside, below = row(cols[j], j), row(cols[j + 1], j), row(cols[j + 1], j + 1)
                recips += [1.0 / pivot, pivot * (1.0 / (pivot * below - beside * beside))]
            a_rows.append(row(a, j))
            q_rows.append(row(q, j))
            c_rows.append([row(cols[k], j) for k in range(SUB)])
            mult = jnp.where(sub > j, cols[j], 0.0) * recips[j]
            a = a - mult * a_rows[j]
            q = q - mult * q_rows[j]
            for k in range(j + 1, SUB):
                cols[k] = cols[k] - mult * c_rows[j][k]
        pivots = cols[0]
        for j in range(1, SUB):
            pivots = jnp.where(sub == j, cols[j], pivots)
        root = lax.rsqrt(pivots)
        upper.append(jnp.where(lane >= sub + SUB * g, a * root, 0.0))
        inverse.append(q * root)
        for m in range(g + 1, per_half if g < per_half else groups):
            a, q = left[m], right[m]
            cols = [column(a, SUB * g + k) for k in range(SUB)]
            for j in range(SUB):
                mult = cols[j] * recips[j]
                a = a - mult * a_rows[j]
                q = q - mult * q_rows[j]
                for k in range(j + 1, SUB):
                    cols[k] = cols[k] - mult * c_rows[j][k]
            left[m], right[m] = a, q
    return jnp.concatenate(upper, 0), jnp.concatenate(inverse, 0)


def unpack_kernel(blocks, core_ref, mine_ref, other_ref, packed_ref, upper_ref, inverse_ref, sems):
    half, first = TILE // 2, blocks * TILE
    core = core_ref[0]
    copies = []
    for lanes in (slice(0, first), slice(first, packed_ref.shape[1])):
        for ref, which in ((mine_ref, core), (other_ref, 1 - core)):
            rows = pl.ds(pl.multiple_of(which * half, half), half)
            copies.append(pltpu.make_async_copy(ref.at[:, lanes], packed_ref.at[rows, lanes], sems.at[len(copies)]))
    for copy in copies:
        copy.start()
    copies[0].wait()
    copies[1].wait()
    upper, inverse = factor_tile(packed_ref[:, :TILE])
    upper_ref[:, :TILE] = upper
    inverse_ref[...] = inverse
    upper_ref[:, TILE:] = dot(inverse, packed_ref[:, TILE:first], 1, 0)
    copies[2].wait()
    copies[3].wait()


def unpack_step(blocks, core, mine, other):
    return pl.pallas_call(
        functools.partial(unpack_kernel, blocks),
        out_shape=(
            jax.ShapeDtypeStruct((TILE, mine.shape[1]), jnp.float32),
            jax.ShapeDtypeStruct((TILE, blocks * TILE), jnp.float32),
            jax.ShapeDtypeStruct((TILE, TILE), jnp.float32),
        ),
        in_specs=[SMEM, ANY, ANY],
        out_specs=(VMEM, VMEM, VMEM),
        scratch_shapes=[pltpu.SemaphoreType.DMA((4,))],
        compiler_params=PARAMS,
        cost_estimate=cost(5),
        name="unpack_step",
    )(core, mine, other)


def factor_kernel(k, blocks, begin, packed_ref, *refs):
    uppers, inverses = refs[:k], refs[k : 2 * k]
    upper_ref, inverse_ref, buf, sem = refs[2 * k :]
    copy = pltpu.make_async_copy(packed_ref.at[:, begin : begin + buf.shape[1]], buf, sem)
    copy.start()
    turned = [jnp.transpose(uppers[j][:, (k - j) * TILE : (k - j + 1) * TILE]) for j in range(k)]
    copy.wait()
    if k:
        total = buf[...]
        for j in range(k):
            total = total - dot(turned[j], uppers[j][:, (k - j) * TILE :], 1, 0)
        buf[...] = total
    upper, inverse = factor_tile(buf[:, :TILE])
    upper_ref[:, :TILE] = upper
    inverse_ref[:, k * TILE :] = inverse
    if k < blocks - 1:
        upper_ref[:, TILE:] = dot(inverse, buf[:, TILE:], 1, 0)
    if k:
        inverse_ref[:, : k * TILE] = jnp.zeros((TILE, k * TILE), jnp.float32)
        for j in range(k):
            inverse_ref[:, : (j + 1) * TILE] += dot_three(turned[j], inverses[j][...])
        inverse_ref[:, : k * TILE] = -dot_three(inverse, inverse_ref[:, : k * TILE])


def factor_step(k, blocks, packed, uppers, inverses):
    begin = sum((blocks - j) * TILE for j in range(k))
    width = (blocks - k) * TILE
    return pl.pallas_call(
        functools.partial(factor_kernel, k, blocks, begin),
        out_shape=(
            jax.ShapeDtypeStruct((TILE, width), jnp.float32),
            jax.ShapeDtypeStruct((TILE, (k + 1) * TILE), jnp.float32),
        ),
        in_specs=[ANY] + [VMEM] * (2 * k),
        out_specs=(VMEM, VMEM),
        scratch_shapes=[pltpu.VMEM((TILE, width), jnp.float32), pltpu.SemaphoreType.DMA],
        compiler_params=PARAMS,
        cost_estimate=cost(7),
        name="factor_step",
    )(packed, *uppers, *inverses)


def tile_rows_kernel(blocks, at_ref, *refs):
    uppers, out_ref = refs[:blocks], refs[blocks]
    at = at_ref[0]
    for j in range(blocks):
        cols = slice(j * TILE, (j + 1) * TILE)

        @pl.when(at >= j)
        def _():
            lanes = pl.ds(pl.multiple_of((at - j) * TILE, TILE), TILE)
            out_ref[:, cols] = jnp.transpose(uppers[j][:, lanes])

        @pl.when(at < j)
        def _():
            out_ref[:, cols] = jnp.zeros((TILE, TILE), jnp.float32)


def tile_rows(at, uppers):
    blocks = len(uppers)
    return pl.pallas_call(
        functools.partial(tile_rows_kernel, blocks),
        out_shape=jax.ShapeDtypeStruct((TILE, blocks * TILE), jnp.float32),
        in_specs=[SMEM] + [VMEM] * blocks,
        out_specs=VMEM,
        compiler_params=PARAMS,
        cost_estimate=cost(1.5),
        name="tile_rows",
    )(at, *uppers)


def assemble(core, mine, other, buf):
    half, start = mine[0].shape[0], 0
    for one, two in zip(mine, other):
        lanes = slice(start, start + one.shape[1])
        buf[pl.ds(pl.multiple_of(core * half, 8), half), lanes] = one[...]
        buf[pl.ds(pl.multiple_of((1 - core) * half, 8), half), lanes] = two[...]
        start = lanes.stop
    return split(buf[...])


def product(high, low, inverse):
    inv_high, inv_low = split(inverse)
    return dot_cols(low, inv_high) + dot_cols(high, inv_low) + dot_cols(high, inv_high)


def below_kernel(blocks, units, core_ref, *refs):
    mine, other = refs[:units], refs[units : 2 * units]
    inverses = refs[2 * units : 2 * units + blocks]
    out_ref, buf = refs[2 * units + blocks :]
    high, low = assemble(core_ref[0], mine, other, buf)
    for j in range(blocks):
        span = min((j + 1) * TILE, buf.shape[1])
        out_ref[:, j * TILE : (j + 1) * TILE] = product(high[:, :span], low[:, :span], inverses[j][:, :span])


def below_rows(core, mine, other, inverses):
    units, blocks = len(mine), len(inverses)
    rows = 2 * mine[0].shape[0]
    return pl.pallas_call(
        functools.partial(below_kernel, blocks, units),
        out_shape=jax.ShapeDtypeStruct((rows, blocks * TILE), jnp.float32),
        in_specs=[SMEM] + [VMEM] * (2 * units + blocks),
        out_specs=VMEM,
        scratch_shapes=[pltpu.VMEM((rows, sum(x.shape[1] for x in mine)), jnp.float32)],
        compiler_params=PARAMS,
        cost_estimate=cost(4),
        name="below_rows",
    )(core, *mine, *other, *inverses)


def last_kernel(begin, count, core_ref, mine_ref, other_ref, *refs):
    inverses = refs[:count]
    part_ref, out_ref, buf, total, sem = refs[count:]
    lanes = slice(begin, begin + total.shape[1])
    load = pltpu.make_async_copy(part_ref.at[:, lanes], total, sem)
    load.start()
    high, low = assemble(core_ref[0], [mine_ref], [other_ref], buf)
    load.wait()
    for n in range(count):
        cols = slice(n * TILE, (n + 1) * TILE)
        span = (n + 1) * TILE
        total[:, cols] += product(high[:, :span], low[:, :span], inverses[n][:, begin : begin + span])
    store = pltpu.make_async_copy(total, out_ref.at[:, lanes], sem)
    store.start()
    store.wait()


def last_rows(core, mine, other, inverses, partial):
    rows, width = 2 * mine.shape[0], mine.shape[1]
    begin, count = partial.shape[1] - width, width // TILE
    return pl.pallas_call(
        functools.partial(last_kernel, begin, count),
        out_shape=jax.ShapeDtypeStruct(partial.shape, jnp.float32),
        in_specs=[SMEM] + [VMEM] * (2 + count) + [ANY],
        out_specs=ANY,
        input_output_aliases={3 + count: 0},
        scratch_shapes=[
            pltpu.VMEM((rows, width), jnp.float32),
            pltpu.VMEM((rows, width), jnp.float32),
            pltpu.SemaphoreType.DMA,
        ],
        compiler_params=PARAMS,
        cost_estimate=cost(2),
        name="last_rows",
    )(core, mine, other, *inverses[-count:], partial)


def after(x, *others):
    return lax.optimization_barrier((x, others))[0] if others else x


def swap_cores(x):
    return lax.ppermute(x, "period", [(0, 1), (1, 0)])


def place():
    row, devices = lax.axis_index("row"), lax.axis_size("row")
    if devices < 4:
        return row
    crossed = lax.div(row, 4) * 4 + lax.rem(row, 2) * 2 + lax.rem(lax.div(row, 2), 2)
    return jnp.where(lax.axis_index("period") == 0, row, crossed)


def swap_places(x, bit):
    devices = lax.axis_size("row")
    pairs = []
    for row in range(devices):
        pairs.append((row, row ^ (1 << bit)))
        crossed = crossed_row(crossed_row(row, devices) ^ (1 << bit), devices)
        pairs.append((devices + row, devices + crossed))
    return lax.ppermute(x, ("period", "row"), pairs)


def my_bit(bit):
    return lax.rem(lax.div(place(), 1 << bit), 2)


def part(x, dims, chosen):
    starts = [chosen.get(bit, 0) for bit in dims] + [0] * (x.ndim - len(dims))
    sizes = [1 if bit in chosen else 2 for bit in dims] + list(x.shape[len(dims) :])
    out = lax.dynamic_slice(x, starts, sizes)
    return out.reshape([2] * sum(bit not in chosen for bit in dims) + list(x.shape[len(dims) :]))


class Halving:
    def __init__(self, mine, other, bits):
        dims = list(reversed(range(bits)))
        self.terms = [(mine, dims), (other, dims)]
        self.chosen = {}
        self.bit = 0

    def total(self, chosen, *deps):
        self.terms[-1] = (after(self.terms[-1][0], *deps), self.terms[-1][1])
        return sum(part(x, dims, {b: v for b, v in chosen.items() if b in dims}) for x, dims in self.terms)

    def send(self, *deps):
        here = my_bit(self.bit)
        sent = self.total({**self.chosen, self.bit: 1 - here}, *deps)
        self.chosen[self.bit] = here
        dims = [b for b in self.terms[0][1] if b not in self.chosen]
        self.terms.append((swap_places(sent, self.bit), dims))
        self.bit += 1
        return sent

    def result(self, *deps):
        return self.total(self.chosen, *deps)


def join(mine, other, here, axis):
    return jnp.where(here == 0, jnp.stack([mine, other], axis), jnp.stack([other, mine], axis))


def shards(linking, tile_mask, scaling, link_diag):
    row_devs = lax.axis_size("row")
    bits = row_devs.bit_length() - 1
    diag_rows = link_diag.shape[0]
    panel = diag_rows * row_devs
    blocks = panel // TILE
    rest_rows = (linking.shape[1] - panel) // row_devs
    row_index = lax.axis_index("row")
    core = lax.axis_index("period")
    core_arg = core.astype(jnp.int32).reshape(1)

    first = jnp.where(core == 0, link_diag, 0.0)
    ridge = lax.dynamic_update_slice(jnp.zeros((panel,), jnp.float32), first, (row_index * diag_rows,))
    diag_send, diag_keep, scaled = diag_products(
        core_arg, tile_mask, scaling.reshape(-1, TILE), ridge.reshape(blocks, TILE), linking, panel
    )
    diag_got = swap_cores(diag_send)

    units = len(WIDTHS)
    unit_lead = (2,) * bits + (rest_rows // 2,)
    rest, made = [], []

    def make_units(first, last, *deps):
        starts = [sum(WIDTHS[:u]) for u in range(units + 1)]
        spans = [slice(starts[u], starts[u + 1]) for u in range(first, last)]
        outs = rest_products(core_arg, tile_mask, after(scaled, *deps), linking, row_devs, spans)
        made.append(outs[0])
        for u in range(first, last):
            send, keep = outs[2 * (u - first)], outs[2 * (u - first) + 1]
            shape = unit_lead + (WIDTHS[u],)
            rest.append(Halving(keep.reshape(shape), swap_cores(send).reshape(shape), bits))

    plan = PLAN if bits == 3 else {"f0": [u for u in range(units) for _ in range(bits)], "end": list(range(units))}
    results = {}

    def more(stage, gate):
        sent = []
        for u in plan.get(stage, []):
            if rest[u].bit < bits:
                sent.append(rest[u].send(*gate))
            else:
                mine = rest[u].result(*gate)
                results[u] = (mine, swap_cores(mine))
                sent.append(mine)
        return sent

    lead = (2,) * bits + (-1, diag_keep.shape[1])
    diag = Halving(diag_keep.reshape(lead), diag_got.reshape(lead), bits)
    gate = []
    for step in range(bits - 1):
        sent = diag.send(*gate)
        if step == 0:
            make_units(0, 1, sent)
        gate = made[-1:] + more(f"s{step}", [sent])
    piece = after(diag.result(), *gate)
    got = swap_places(piece, bits - 1)
    make_units(1, units, piece)
    gate = made[-1:] + more("x", [piece])
    early = [r.terms[-1][0] for r in rest if r.bit]
    piece = piece + after(got, *gate)
    for step in reversed(range(bits - 1)):
        piece = after(piece, *gate)
        if step == bits - 2:
            piece = after(piece, *early)
        gate = more(f"d{step}", [piece])
        piece = join(piece, swap_places(piece, step), my_bit(step), bits - 1 - step)
    half = after(piece.reshape(diag_keep.shape), *gate)
    packed = (half, swap_cores(half))

    uppers, inverses = [], []
    gate = more("f", [half])
    for k in range(blocks):
        inputs = after((packed, uppers, inverses), *gate)
        if k == 0:
            packed, upper, inverse = unpack_step(blocks, core_arg, *inputs[0])
        else:
            upper, inverse = factor_step(k, blocks, *inputs)
        uppers.append(upper)
        inverses.append(inverse)
        gate = more(f"f{k}", [upper])
    at = row_index * diag_rows
    rows = tile_rows((at // TILE).astype(jnp.int32).reshape(1), uppers)
    my_factor = lax.dynamic_slice_in_dim(rows, at % TILE, diag_rows, 0)
    more("end", [upper])
    mine, other = zip(*[results[u] for u in range(units)])
    below = below_rows(core_arg, mine[:-1], other[:-1], inverses)
    below = last_rows(core_arg, mine[-1], other[-1], inverses, below)
    return my_factor, below


def solution(mesh):
    whole = P(("inst", "period", "row"), None)
    out = P(("inst", "row"), None)
    return jax.shard_map(
        shards,
        mesh=mesh,
        in_specs=(whole, whole, P(("inst", "period", "row")), P(("inst", "row"))),
        out_specs=(out, out),
        check_vma=False,
    )
```

```python
import functools

import jax
import jax.numpy as jnp
from jax import lax
from jax.experimental import pallas as pl
from jax.experimental.pallas import tpu as pltpu
from jax.sharding import PartitionSpec as P

TILE = 128
SUB = 8
HIGH = lax.Precision.HIGHEST
VMEM = pl.BlockSpec(memory_space=pltpu.VMEM)
SMEM = pl.BlockSpec(memory_space=pltpu.SMEM)
ANY = pl.BlockSpec(memory_space=pl.ANY)
WIDTHS = (384, 384, 256)
PLAN = {"x": [0], "f": [1], "f0": [0], "f1": [2], "f2": [0, 1], "f4": [2, 1], "f5": [2, 0], "end": [1, 2]}
PARAMS = pltpu.CompilerParams(vmem_limit_bytes=48 << 20)


def cost(us):
    return pl.CostEstimate(flops=int(us * 1.1e9), bytes_accessed=int(us * 3.5e6), transcendentals=0)


def dot(a, b, contract_a, contract_b):
    return lax.dot_general(
        a, b, (((contract_a,), (contract_b,)), ((), ())), precision=HIGH, preferred_element_type=jnp.float32
    )


def dot_rows(a, b):
    return lax.dot_general(a, b, (((0,), (0,)), ((), ())), preferred_element_type=jnp.float32)


def dot_cols(a, b):
    return lax.dot_general(a, b, (((1,), (1,)), ((), ())), preferred_element_type=jnp.float32)


def split(x):
    high = x.astype(jnp.bfloat16)
    return high, (x - high.astype(jnp.float32)).astype(jnp.bfloat16)


def dot_three(a, b):
    (a_high, a_low), (b_high, b_low) = split(a), split(b)

    def one(x, y):
        return jnp.dot(x, y, preferred_element_type=jnp.float32)

    return one(a_low, b_high) + one(a_high, b_low) + one(a_high, b_high)


def crossed_row(index, devices):
    if devices < 4:
        return index
    return index // 4 * 4 + index % 2 * 2 + index // 2 % 2


def diag_kernel(core_ref, mask_ref, scale_ref, ridge_ref, lin_ref, send_ref, keep_ref, scaled_ref, masked, buf):
    rows, width = lin_ref.shape
    blocks = width // TILE
    half = TILE // 2
    for t in range(rows // TILE):
        lanes = slice(t * TILE, (t + 1) * TILE)
        factor = jnp.transpose(jnp.broadcast_to(scale_ref[t : t + 1, :], (TILE, TILE)))
        for i in range(blocks):
            cols = slice(i * TILE, (i + 1) * TILE)
            tile = lin_ref[lanes, cols].astype(jnp.float32) * mask_ref[t, i].astype(jnp.float32)
            masked[lanes, cols] = tile.astype(jnp.bfloat16)
            scaled_ref[lanes, cols] = (factor * tile).astype(jnp.bfloat16)
    eye = lax.broadcasted_iota(jnp.int32, (TILE, TILE), 0) == lax.broadcasted_iota(jnp.int32, (TILE, TILE), 1)
    start = 0
    for j in range(blocks):
        first = slice(j * TILE, (j + 1) * TILE)
        span = (blocks - j) * TILE
        buf[:, start : start + span] = 0.5 * (
            dot_rows(scaled_ref[:, first], masked[:, j * TILE :]) + dot_rows(masked[:, first], scaled_ref[:, j * TILE :])
        )
        buf[:, start : start + TILE] += jnp.where(eye, ridge_ref[j : j + 1, :], 0.0)
        start += span
    core = core_ref[0]
    keep_ref[...] = buf[pl.ds(pl.multiple_of(core * half, half), half), :]
    send_ref[...] = buf[pl.ds(pl.multiple_of((1 - core) * half, half), half), :]


def diag_products(core, tile_mask, scaling, ridge, linking, width):
    rows = linking.shape[0]
    blocks = width // TILE
    packed = blocks * (blocks + 1) // 2 * TILE
    half = jax.ShapeDtypeStruct((TILE // 2, packed), jnp.float32)
    return pl.pallas_call(
        diag_kernel,
        grid=(1,),
        out_shape=(half, half, jax.ShapeDtypeStruct((rows, width), jnp.bfloat16)),
        in_specs=[SMEM, SMEM, VMEM, VMEM, pl.BlockSpec((rows, width), lambda g: (0, 0))],
        out_specs=(VMEM, VMEM, VMEM),
        scratch_shapes=[pltpu.VMEM((rows, width), jnp.bfloat16), pltpu.VMEM((TILE, packed), jnp.float32)],
        compiler_params=PARAMS,
        cost_estimate=cost(5),
        name="diag_products",
    )(core, tile_mask, scaling, ridge, linking)


def rest_kernel(first, spans, count, core_ref, mask_ref, scaled_ref, *refs):
    lin_refs = refs[:count]
    out_refs = refs[count : count + 2 * len(spans)]
    masked, buf = refs[count + 2 * len(spans) :]
    rows, width = lin_refs[0].shape
    devices, half = out_refs[0].shape[:2]
    for n in range(count):
        for i in range(width // TILE):
            cols = slice(i * TILE, (i + 1) * TILE)
            to = slice(n * width + i * TILE, n * width + (i + 1) * TILE)
            for t in range(rows // TILE):
                down = slice(t * TILE, (t + 1) * TILE)
                flag = mask_ref[t, first + n * (width // TILE) + i].astype(jnp.float32)
                masked[down, to] = (lin_refs[n][down, cols].astype(jnp.float32) * flag).astype(jnp.bfloat16)
    start = spans[0].start
    buf[...] = dot_rows(masked[...], scaled_ref[:, start : spans[-1].stop])
    core = core_ref[0]
    for n, span in enumerate(spans):
        lanes = slice(span.start - start, span.stop - start)
        for i in range(devices):
            straight, crossed = 2 * half * i, 2 * half * crossed_row(i, devices)
            send = jnp.where(core == 0, crossed + half, straight)
            keep = jnp.where(core == 0, straight, crossed + half)
            out_refs[2 * n][i] = buf[pl.ds(pl.multiple_of(send, half), half), lanes]
            out_refs[2 * n + 1][i] = buf[pl.ds(pl.multiple_of(keep, half), half), lanes]


def rest_products(core, tile_mask, scaled, linking, devices, spans):
    rows, panel = scaled.shape
    below = linking.shape[1] - panel
    count = below // panel
    half = below // devices // 2
    outs = [jax.ShapeDtypeStruct((devices, half, span.stop - span.start), jnp.float32) for span in spans for _ in range(2)]
    return pl.pallas_call(
        functools.partial(rest_kernel, panel // TILE, spans, count),
        grid=(1,),
        out_shape=outs,
        in_specs=[SMEM, SMEM, VMEM]
        + [pl.BlockSpec((rows, panel), functools.partial(lambda n, g: (0, n + 1), n)) for n in range(count)],
        out_specs=[VMEM] * len(outs),
        scratch_shapes=[
            pltpu.VMEM((rows, below), jnp.bfloat16),
            pltpu.VMEM((below, spans[-1].stop - spans[0].start), jnp.float32),
        ],
        compiler_params=PARAMS,
        cost_estimate=cost(6),
        name="rest_products",
    )(core, tile_mask, scaled, *([linking] * count))


def factor_tile(block):
    groups, per_half = TILE // SUB, TILE // SUB // 2
    sub = lax.broadcasted_iota(jnp.int32, (SUB, TILE), 0)
    lane = lax.broadcasted_iota(jnp.int32, (SUB, TILE), 1)

    def column(x, at):
        return jnp.broadcast_to(x[:, at : at + 1], (SUB, TILE))

    def row(x, at):
        return jnp.broadcast_to(x[at : at + 1, :], (SUB, TILE))

    left = [block[SUB * g : SUB * (g + 1), :] for g in range(groups)]
    right = [jnp.where(lane == sub + SUB * g, 1.0, 0.0).astype(jnp.float32) for g in range(groups)]
    upper, inverse = [], []
    for g in range(groups):
        if g == per_half:
            both = jnp.concatenate([jnp.concatenate(upper, 0), jnp.concatenate(inverse, 0)], 1)
            later = jnp.transpose(both[:, :TILE])[SUB * g :, :]
            update = dot(later, both, 1, 0)
            for m in range(g, groups):
                at = slice(SUB * (m - g), SUB * (m - g + 1))
                left[m], right[m] = left[m] - update[at, :TILE], right[m] - update[at, TILE:]
        a, q = left[g], right[g]
        cols = [column(a, SUB * g + k) for k in range(SUB)]
        recips, a_rows, q_rows, c_rows = [], [], [], []
        for j in range(SUB):
            if j % 2 == 0:
                pivot, beside, below = row(cols[j], j), row(cols[j + 1], j), row(cols[j + 1], j + 1)
                recips += [1.0 / pivot, pivot * (1.0 / (pivot * below - beside * beside))]
            a_rows.append(row(a, j))
            q_rows.append(row(q, j))
            c_rows.append([row(cols[k], j) for k in range(SUB)])
            mult = jnp.where(sub > j, cols[j], 0.0) * recips[j]
            a = a - mult * a_rows[j]
            q = q - mult * q_rows[j]
            for k in range(j + 1, SUB):
                cols[k] = cols[k] - mult * c_rows[j][k]
        pivots = cols[0]
        for j in range(1, SUB):
            pivots = jnp.where(sub == j, cols[j], pivots)
        root = lax.rsqrt(pivots)
        upper.append(jnp.where(lane >= sub + SUB * g, a * root, 0.0))
        inverse.append(q * root)
        for m in range(g + 1, per_half if g < per_half else groups):
            a, q = left[m], right[m]
            cols = [column(a, SUB * g + k) for k in range(SUB)]
            for j in range(SUB):
                mult = cols[j] * recips[j]
                a = a - mult * a_rows[j]
                q = q - mult * q_rows[j]
                for k in range(j + 1, SUB):
                    cols[k] = cols[k] - mult * c_rows[j][k]
            left[m], right[m] = a, q
    return jnp.concatenate(upper, 0), jnp.concatenate(inverse, 0)


def unpack_kernel(blocks, core_ref, mine_ref, other_ref, packed_ref, upper_ref, inverse_ref, sems):
    half, first = TILE // 2, blocks * TILE
    core = core_ref[0]
    copies = []
    for lanes in (slice(0, first), slice(first, packed_ref.shape[1])):
        for ref, which in ((mine_ref, core), (other_ref, 1 - core)):
            rows = pl.ds(pl.multiple_of(which * half, half), half)
            copies.append(pltpu.make_async_copy(ref.at[:, lanes], packed_ref.at[rows, lanes], sems.at[len(copies)]))
    for copy in copies:
        copy.start()
    copies[0].wait()
    copies[1].wait()
    upper, inverse = factor_tile(packed_ref[:, :TILE])
    upper_ref[:, :TILE] = upper
    inverse_ref[...] = inverse
    upper_ref[:, TILE:] = dot(inverse, packed_ref[:, TILE:first], 1, 0)
    copies[2].wait()
    copies[3].wait()


def unpack_step(blocks, core, mine, other):
    return pl.pallas_call(
        functools.partial(unpack_kernel, blocks),
        out_shape=(
            jax.ShapeDtypeStruct((TILE, mine.shape[1]), jnp.float32),
            jax.ShapeDtypeStruct((TILE, blocks * TILE), jnp.float32),
            jax.ShapeDtypeStruct((TILE, TILE), jnp.float32),
        ),
        in_specs=[SMEM, ANY, ANY],
        out_specs=(VMEM, VMEM, VMEM),
        scratch_shapes=[pltpu.SemaphoreType.DMA((4,))],
        compiler_params=PARAMS,
        cost_estimate=cost(5),
        name="unpack_step",
    )(core, mine, other)


def factor_kernel(k, blocks, begin, packed_ref, *refs):
    uppers, inverses = refs[:k], refs[k : 2 * k]
    upper_ref, inverse_ref, buf, sem = refs[2 * k :]
    copy = pltpu.make_async_copy(packed_ref.at[:, begin : begin + buf.shape[1]], buf, sem)
    copy.start()
    turned = [jnp.transpose(uppers[j][:, (k - j) * TILE : (k - j + 1) * TILE]) for j in range(k)]
    copy.wait()
    if k:
        total = buf[...]
        for j in range(k):
            total = total - dot(turned[j], uppers[j][:, (k - j) * TILE :], 1, 0)
        buf[...] = total
    upper, inverse = factor_tile(buf[:, :TILE])
    upper_ref[:, :TILE] = upper
    inverse_ref[:, k * TILE :] = inverse
    if k < blocks - 1:
        upper_ref[:, TILE:] = dot(inverse, buf[:, TILE:], 1, 0)
    if k:
        inverse_ref[:, : k * TILE] = jnp.zeros((TILE, k * TILE), jnp.float32)
        for j in range(k):
            inverse_ref[:, : (j + 1) * TILE] += dot_three(turned[j], inverses[j][...])
        inverse_ref[:, : k * TILE] = -dot_three(inverse, inverse_ref[:, : k * TILE])


def factor_step(k, blocks, packed, uppers, inverses):
    begin = sum((blocks - j) * TILE for j in range(k))
    width = (blocks - k) * TILE
    return pl.pallas_call(
        functools.partial(factor_kernel, k, blocks, begin),
        out_shape=(
            jax.ShapeDtypeStruct((TILE, width), jnp.float32),
            jax.ShapeDtypeStruct((TILE, (k + 1) * TILE), jnp.float32),
        ),
        in_specs=[ANY] + [VMEM] * (2 * k),
        out_specs=(VMEM, VMEM),
        scratch_shapes=[pltpu.VMEM((TILE, width), jnp.float32), pltpu.SemaphoreType.DMA],
        compiler_params=PARAMS,
        cost_estimate=cost(7),
        name="factor_step",
    )(packed, *uppers, *inverses)


def tile_rows_kernel(blocks, at_ref, *refs):
    uppers, out_ref = refs[:blocks], refs[blocks]
    at = at_ref[0]
    for j in range(blocks):
        cols = slice(j * TILE, (j + 1) * TILE)

        @pl.when(at >= j)
        def _():
            lanes = pl.ds(pl.multiple_of((at - j) * TILE, TILE), TILE)
            out_ref[:, cols] = jnp.transpose(uppers[j][:, lanes])

        @pl.when(at < j)
        def _():
            out_ref[:, cols] = jnp.zeros((TILE, TILE), jnp.float32)


def tile_rows(at, uppers):
    blocks = len(uppers)
    return pl.pallas_call(
        functools.partial(tile_rows_kernel, blocks),
        out_shape=jax.ShapeDtypeStruct((TILE, blocks * TILE), jnp.float32),
        in_specs=[SMEM] + [VMEM] * blocks,
        out_specs=VMEM,
        compiler_params=PARAMS,
        cost_estimate=cost(1.5),
        name="tile_rows",
    )(at, *uppers)


def assemble(core, mine, other, buf):
    half, start = mine[0].shape[0], 0
    for one, two in zip(mine, other):
        lanes = slice(start, start + one.shape[1])
        buf[pl.ds(pl.multiple_of(core * half, 8), half), lanes] = one[...]
        buf[pl.ds(pl.multiple_of((1 - core) * half, 8), half), lanes] = two[...]
        start = lanes.stop
    return split(buf[...])


def product(high, low, inverse):
    inv_high, inv_low = split(inverse)
    return dot_cols(low, inv_high) + dot_cols(high, inv_low) + dot_cols(high, inv_high)


def below_kernel(blocks, units, core_ref, *refs):
    mine, other = refs[:units], refs[units : 2 * units]
    inverses = refs[2 * units : 2 * units + blocks]
    out_ref, buf = refs[2 * units + blocks :]
    high, low = assemble(core_ref[0], mine, other, buf)
    for j in range(blocks):
        span = min((j + 1) * TILE, buf.shape[1])
        out_ref[:, j * TILE : (j + 1) * TILE] = product(high[:, :span], low[:, :span], inverses[j][:, :span])


def below_rows(core, mine, other, inverses):
    units, blocks = len(mine), len(inverses)
    rows = 2 * mine[0].shape[0]
    return pl.pallas_call(
        functools.partial(below_kernel, blocks, units),
        out_shape=jax.ShapeDtypeStruct((rows, blocks * TILE), jnp.float32),
        in_specs=[SMEM] + [VMEM] * (2 * units + blocks),
        out_specs=VMEM,
        scratch_shapes=[pltpu.VMEM((rows, sum(x.shape[1] for x in mine)), jnp.float32)],
        compiler_params=PARAMS,
        cost_estimate=cost(4),
        name="below_rows",
    )(core, *mine, *other, *inverses)


def last_kernel(begin, count, core_ref, mine_ref, other_ref, *refs):
    inverses = refs[:count]
    part_ref, out_ref, buf, total, sem = refs[count:]
    lanes = slice(begin, begin + total.shape[1])
    load = pltpu.make_async_copy(part_ref.at[:, lanes], total, sem)
    load.start()
    high, low = assemble(core_ref[0], [mine_ref], [other_ref], buf)
    load.wait()
    for n in range(count):
        cols = slice(n * TILE, (n + 1) * TILE)
        span = (n + 1) * TILE
        total[:, cols] += product(high[:, :span], low[:, :span], inverses[n][:, begin : begin + span])
    store = pltpu.make_async_copy(total, out_ref.at[:, lanes], sem)
    store.start()
    store.wait()


def last_rows(core, mine, other, inverses, partial):
    rows, width = 2 * mine.shape[0], mine.shape[1]
    begin, count = partial.shape[1] - width, width // TILE
    return pl.pallas_call(
        functools.partial(last_kernel, begin, count),
        out_shape=jax.ShapeDtypeStruct(partial.shape, jnp.float32),
        in_specs=[SMEM] + [VMEM] * (2 + count) + [ANY],
        out_specs=ANY,
        input_output_aliases={3 + count: 0},
        scratch_shapes=[
            pltpu.VMEM((rows, width), jnp.float32),
            pltpu.VMEM((rows, width), jnp.float32),
            pltpu.SemaphoreType.DMA,
        ],
        compiler_params=PARAMS,
        cost_estimate=cost(2),
        name="last_rows",
    )(core, mine, other, *inverses[-count:], partial)


def after(x, *others):
    return lax.optimization_barrier((x, others))[0] if others else x


def swap_cores(x):
    return lax.ppermute(x, "period", [(0, 1), (1, 0)])


def place():
    row, devices = lax.axis_index("row"), lax.axis_size("row")
    if devices < 4:
        return row
    crossed = lax.div(row, 4) * 4 + lax.rem(row, 2) * 2 + lax.rem(lax.div(row, 2), 2)
    return jnp.where(lax.axis_index("period") == 0, row, crossed)


def swap_places(x, bit):
    devices = lax.axis_size("row")
    pairs = []
    for row in range(devices):
        pairs.append((row, row ^ (1 << bit)))
        crossed = crossed_row(crossed_row(row, devices) ^ (1 << bit), devices)
        pairs.append((devices + row, devices + crossed))
    return lax.ppermute(x, ("period", "row"), pairs)


def my_bit(bit):
    return lax.rem(lax.div(place(), 1 << bit), 2)


def part(x, dims, chosen):
    starts = [chosen.get(bit, 0) for bit in dims] + [0] * (x.ndim - len(dims))
    sizes = [1 if bit in chosen else 2 for bit in dims] + list(x.shape[len(dims) :])
    out = lax.dynamic_slice(x, starts, sizes)
    return out.reshape([2] * sum(bit not in chosen for bit in dims) + list(x.shape[len(dims) :]))


class Halving:
    def __init__(self, mine, other, bits):
        dims = list(reversed(range(bits)))
        self.terms = [(mine, dims), (other, dims)]
        self.chosen = {}
        self.bit = 0

    def total(self, chosen, *deps):
        self.terms[-1] = (after(self.terms[-1][0], *deps), self.terms[-1][1])
        return sum(part(x, dims, {b: v for b, v in chosen.items() if b in dims}) for x, dims in self.terms)

    def send(self, *deps):
        here = my_bit(self.bit)
        sent = self.total({**self.chosen, self.bit: 1 - here}, *deps)
        self.chosen[self.bit] = here
        dims = [b for b in self.terms[0][1] if b not in self.chosen]
        self.terms.append((swap_places(sent, self.bit), dims))
        self.bit += 1
        return sent

    def result(self, *deps):
        return self.total(self.chosen, *deps)


def join(mine, other, here, axis):
    return jnp.where(here == 0, jnp.stack([mine, other], axis), jnp.stack([other, mine], axis))


def shards(linking, tile_mask, scaling, link_diag):
    row_devs = lax.axis_size("row")
    bits = row_devs.bit_length() - 1
    diag_rows = link_diag.shape[0]
    panel = diag_rows * row_devs
    blocks = panel // TILE
    rest_rows = (linking.shape[1] - panel) // row_devs
    row_index = lax.axis_index("row")
    core = lax.axis_index("period")
    core_arg = core.astype(jnp.int32).reshape(1)

    first = jnp.where(core == 0, link_diag, 0.0)
    ridge = lax.dynamic_update_slice(jnp.zeros((panel,), jnp.float32), first, (row_index * diag_rows,))
    diag_send, diag_keep, scaled = diag_products(
        core_arg, tile_mask, scaling.reshape(-1, TILE), ridge.reshape(blocks, TILE), linking, panel
    )
    diag_got = swap_cores(diag_send)

    units = len(WIDTHS)
    unit_lead = (2,) * bits + (rest_rows // 2,)
    rest, made = [], []

    def make_units(first, last, *deps):
        starts = [sum(WIDTHS[:u]) for u in range(units + 1)]
        spans = [slice(starts[u], starts[u + 1]) for u in range(first, last)]
        outs = rest_products(core_arg, tile_mask, after(scaled, *deps), linking, row_devs, spans)
        made.append(outs[0])
        for u in range(first, last):
            send, keep = outs[2 * (u - first)], outs[2 * (u - first) + 1]
            shape = unit_lead + (WIDTHS[u],)
            rest.append(Halving(keep.reshape(shape), swap_cores(send).reshape(shape), bits))

    plan = PLAN if bits == 3 else {"f0": [u for u in range(units) for _ in range(bits)], "end": list(range(units))}
    results = {}

    def more(stage, gate):
        sent = []
        for u in plan.get(stage, []):
            if rest[u].bit < bits:
                sent.append(rest[u].send(*gate))
            else:
                mine = rest[u].result(*gate)
                results[u] = (mine, swap_cores(mine))
                sent.append(mine)
        return sent

    lead = (2,) * bits + (-1, diag_keep.shape[1])
    diag = Halving(diag_keep.reshape(lead), diag_got.reshape(lead), bits)
    gate = []
    for step in range(bits - 1):
        sent = diag.send(*gate)
        if step == 0:
            make_units(0, 1, sent)
        gate = made[-1:] + more(f"s{step}", [sent])
    piece = after(diag.result(), *gate)
    got = swap_places(piece, bits - 1)
    make_units(1, units, piece)
    gate = made[-1:] + more("x", [piece])
    early = [r.terms[-1][0] for r in rest if r.bit]
    piece = piece + after(got, *gate)
    for step in reversed(range(bits - 1)):
        piece = after(piece, *gate)
        if step == bits - 2:
            piece = after(piece, *early)
        gate = more(f"d{step}", [piece])
        piece = join(piece, swap_places(piece, step), my_bit(step), bits - 1 - step)
    half = after(piece.reshape(diag_keep.shape), *gate)
    packed = (half, swap_cores(half))

    uppers, inverses = [], []
    gate = more("f", [half])
    for k in range(blocks):
        inputs = after((packed, uppers, inverses), *gate)
        if k == 0:
            packed, upper, inverse = unpack_step(blocks, core_arg, *inputs[0])
        else:
            upper, inverse = factor_step(k, blocks, *inputs)
        uppers.append(upper)
        inverses.append(inverse)
        gate = more(f"f{k}", [upper])
    at = row_index * diag_rows
    rows = tile_rows((at // TILE).astype(jnp.int32).reshape(1), uppers)
    my_factor = lax.dynamic_slice_in_dim(rows, at % TILE, diag_rows, 0)
    more("end", [upper])
    mine, other = zip(*[results[u] for u in range(units)])
    below = below_rows(core_arg, mine[:-1], other[:-1], inverses)
    below = last_rows(core_arg, mine[-1], other[-1], inverses, below)
    return my_factor, below


def solution(mesh):
    whole = P(("inst", "period", "row"), None)
    out = P(("inst", "row"), None)
    return jax.shard_map(
        shards,
        mesh=mesh,
        in_specs=(whole, whole, P(("inst", "period", "row")), P(("inst", "row"))),
        out_specs=(out, out),
        check_vma=False,
    )
```
